32 devices in a mesh: dp: 8 (over z, core), tensor: 4 (over y, x).
Axes of the slice: x: 2, y: 2, z: 4, core: 2. Of those that a mesh axis runs over, the one named last changes fastest.
Arguments:
- out_grad: bfloat16 [2048, 4096], P('dp'), may hold values from -8 to 8
- hidden_act: bfloat16 [2048, 15360], P('dp', 'tensor'), may hold values from -6 to 6
- log_ratio: float32 [64], P('dp'), may hold values from -40 to 40
- pair_order: int32 [8, 8], P('dp'), may hold values from 0 to 7, each once within a row
- seq_len: int32 [64], P('dp'), may hold values from 1 to 32, 1280 in all
- master: float32 [4096, 15360], P('dp', 'tensor'), may hold values from -0.046875 to 0.046875
- moment: float32 [4096, 15360], P('dp', 'tensor'), may hold values from -6 to 6
- second: float32 [4096, 15360], P('dp', 'tensor'), may hold values from 0.005 to 0.08
- next_act: bfloat16 [4096, 15360], P('dp', 'tensor'), may hold values from -6 to 6
Outputs:
- new_master: float32 [4096, 15360], P('dp', 'tensor')
- new_moment: float32 [4096, 15360], P('dp', 'tensor')
- new_second: float32 [4096, 15360], P('dp', 'tensor')
- update: float32 [4096, 15360], P('dp', 'tensor')
- next_out: bfloat16 [4096, 4096], P('dp', 'tensor')
The draws below stay inside these ranges and needn't reach their ends.
Inputs may be any that keep to these rules, and one draw needn't show every extreme that they name: Each row of pair_order holds every number below 8 once.
All inputs are finite; a program needn't handle non-finite values. No bound on the sum of `seq_len` on one device may be relied on, other than what follows from the above.
Results may differ from the reference program's by a relative error of at most 0.02.
Values may be sent and summed in bfloat16 or wider, within the bound.
No kernel may reach another device: no remote copies, remote signals or barrier semaphores. Data moves between devices by JAX's collectives and lax.ppermute only.
A program may use at most 192 MiB of HBM per device.

```python
import math
import jax
import jax.numpy as jnp
import numpy as np
from jax import lax

D = 4096
FF = 15360
LEN = 32
TOK_DEV = 256
SEQ_DEV = 8
SEQS = 64
TOKENS = 2048
NEXT = 4096
N_DP = 8
N_TENSOR = 4


def with_spikes(array, stream_key, source, target, shards_of, factor):
    def block_of(dim):
        return (jnp.arange(array.shape[dim]) // (array.shape[dim] // shards_of)).reshape((-1,) + (1,) * (array.ndim - 1 - dim))

    one_side = jax.random.permutation(stream_key, shards_of)[block_of(target)]
    other_side = (block_of(target) + shards_of // 2) % shards_of
    return jnp.where((block_of(source) == one_side) | (block_of(source) == other_side), factor * array, array)


def block_levels(rng, shape, split, low, largest):
    factor_of = 1.0
    for dim, blocks in split:
        draws = jax.random.uniform(jax.random.fold_in(jax.random.fold_in(rng, 6), dim), (blocks,), jnp.float32, low / len(split), largest / len(split))
        factor_of = factor_of * jnp.repeat(jnp.exp(draws), shape[dim] // blocks).reshape((-1,) + (1,) * (len(shape) - 1 - dim))
    return factor_of


def split_up(amount, total, reach, skew):
    loads = [(1 << 20) // math.isqrt(standing ** skew) + 1 for standing in range(2, amount + 1)]
    rest, counts = total - reach - (amount - 1), [1] * (amount - 1)
    while rest > 0:
        candidates = [i for i in range(amount - 1) if counts[i] < reach]
        mass, remaining = sum([loads[i] for i in candidates]), rest
        for i in candidates:
            addition = min(reach - counts[i], max(1, remaining * loads[i] // mass), rest)
            counts[i] = counts[i] + addition
            rest = rest - addition
    return np.array([reach] + counts)


def ragged_sizes(rng, count, total, bound, slope):
    if count == 2:
        one = jax.random.randint(rng, (), max(1, total - bound), min(bound, total - 1) + 1)
        return jnp.stack([one, total - one])
    sizes = jnp.asarray(split_up(count, total, bound, slope), jnp.int32)
    twos = (count - 1) // 2
    donor, sink = sizes[1:1 + 2 * twos:2], sizes[2:2 + 2 * twos:2]
    slack = jnp.minimum(donor - 1, bound - sink)
    moved = jax.random.randint(jax.random.fold_in(rng, 1), (twos,), 0, 1 << 20) % (slack + 1)
    sizes = sizes.at[1:1 + 2 * twos:2].set(donor - moved).at[2:2 + 2 * twos:2].set(sink + moved)
    return sizes[jax.random.permutation(jax.random.fold_in(rng, 2), count)]


def scatter_about(rng, extent, deviation, bound, cuts=(), kind=jnp.bfloat16):
    drawn = jax.random.normal(rng, extent, jnp.float32) * deviation
    if len(cuts) > 0:
        drawn = block_levels(rng, extent, cuts, -0.22, 0.18) * drawn
    return jnp.clip(drawn, min=-bound, max=bound).astype(kind)


def noise_with(rng, shape, deviation, reach, cuts, heavy, kind=jnp.bfloat16):
    entries = deviation * jax.random.normal(rng, shape, jnp.float32)
    if cuts:
        entries = entries * block_levels(rng, shape, cuts, -0.22, 0.18)
    return jnp.clip(with_spikes(entries, jax.random.fold_in(rng, 3), *heavy), -reach, reach).astype(kind)


def setup_inputs(seed: int = 0) -> dict:
    streams_of = jax.random.split(jax.random.key(seed), 10)
    out_grad = noise_with(streams_of[0], (TOKENS, D), 1.0, 8.0, ((0, 8),), (0, 1, 8, 2.0))
    hidden_act = scatter_about(streams_of[1], (TOKENS, FF), 1.0, 6.0, ((0, 8), (1, 4)))
    log_ratio = scatter_about(streams_of[2], (SEQS,), 10.0, 40.0, ((0, 8),), jnp.float32)
    pair_order = jax.vmap(lambda own: jax.random.permutation(own, SEQ_DEV))(jax.random.split(streams_of[3], N_DP)).reshape((N_DP, SEQ_DEV)).astype(jnp.int32)
    seq_len = ragged_sizes(streams_of[4], SEQS, 20 * SEQS, LEN, 0).astype(jnp.int32)
    master = scatter_about(streams_of[5], (D, FF), FF ** -0.5, 0.046875, ((0, 8), (1, 4)), jnp.float32)
    moment = scatter_about(streams_of[6], (D, FF), 1.0, 6.0, ((0, 8), (1, 4)), jnp.float32)
    second = jnp.clip(jnp.exp(math.log(0.08) - 2.7725887 * jax.random.uniform(streams_of[7], (D, FF), jnp.float32) ** block_levels(streams_of[7], (D, FF), ((0, 8), (1, 4)), -0.2, 0.2)), 0.005, 0.08)
    next_act = scatter_about(streams_of[8], (NEXT, FF), 1.0, 6.0, ((0, 8), (1, 4)))
    return dict(out_grad=out_grad, hidden_act=hidden_act, log_ratio=log_ratio, pair_order=pair_order, seq_len=seq_len, master=master, moment=moment, second=second, next_act=next_act)


beta_dpo = 0.1
beta_one = 0.9
beta_two = 0.999
bias_one = 1.0 - 0.9 ** 10
bias_two = 1.0 - 0.999 ** 10
adam_eps = 1e-08
rate_learn = 0.001

def row_factors(ratios, pair_row, lengths):
    seq_count = ratios.shape[0]
    seq_slots = jnp.arange(seq_count, dtype=jnp.int32)
    chosen = pair_row[0::2]
    rejected = pair_row[1::2]
    pick_chosen = (chosen[:, None] == seq_slots[None, :]).astype(jnp.float32)
    pick_rejected = (rejected[:, None] == seq_slots[None, :]).astype(jnp.float32)
    margin = beta_dpo * (lax.optimization_barrier(jnp.sum(pick_chosen * ratios[None, :], axis=1)) - lax.optimization_barrier(jnp.sum(pick_rejected * ratios[None, :], axis=1)))
    weight = beta_dpo * jax.nn.sigmoid(-margin)
    coefficient = lax.optimization_barrier(jnp.sum(weight[:, None] * (pick_rejected - pick_chosen), axis=0))
    position = jnp.arange(LEN, dtype=jnp.int32)
    in_length = (position[None, :] < lengths[:, None]).astype(jnp.float32)
    return coefficient[:, None] * in_length

def adam_step(grad, master, moment, second):
    new_moment = beta_one * moment + (1.0 - beta_one) * grad
    new_second = beta_two * second + (1.0 - beta_two) * grad * grad
    update = new_moment / bias_one / (jnp.sqrt(new_second / bias_two) + adam_eps)
    new_master = master - rate_learn * update
    return (new_master, new_moment, new_second, update)

def reference(out_grad, hidden_act, log_ratio, pair_order, seq_len, master, moment, second, next_act):
    factors = jax.vmap(row_factors)(log_ratio.reshape(N_DP, SEQ_DEV), pair_order, seq_len.reshape(N_DP, SEQ_DEV))
    scaled = (out_grad.astype(jnp.float32) * factors.reshape(-1)[:, None]).astype(jnp.bfloat16)
    grad = jnp.zeros((D, FF), jnp.float32)
    for shard in range(N_DP):
        rows_grad = scaled[shard * TOK_DEV:(shard + 1) * TOK_DEV]
        rows_act = hidden_act[shard * TOK_DEV:(shard + 1) * TOK_DEV]
        term = jnp.dot(rows_grad.T, rows_act, preferred_element_type=jnp.float32)
        grad = grad + lax.optimization_barrier(term.astype(jnp.bfloat16)).astype(jnp.float32)
    new_master, new_moment, new_second, update = adam_step(grad, master, moment, second)
    weights = new_master.astype(jnp.bfloat16)
    block_width = FF // N_TENSOR
    total_next = jnp.zeros((NEXT, D), jnp.float32)
    for column_block in range(N_TENSOR):
        lower = column_block * block_width
        partial_next = jnp.dot(next_act[:, lower:lower + block_width], weights[:, lower:lower + block_width].T, preferred_element_type=jnp.float32)
        total_next = total_next + lax.optimization_barrier(partial_next.astype(jnp.bfloat16)).astype(jnp.float32)
    next_out = total_next.astype(jnp.bfloat16)
    return (new_master, new_moment, new_second, update, next_out)
```

```python
import functools

import jax
import jax.numpy as jnp
from jax import lax
from jax.experimental import pallas as pl
from jax.experimental.pallas import tpu as pltpu
from jax.sharding import PartitionSpec as P

LEN = 32


beta_dpo = 0.1
beta_one = 0.9
beta_two = 0.999
bias_one = 1.0 - 0.9**10
bias_two = 1.0 - 0.999**10
adam_eps = 1e-08
rate_learn = 0.001

ROW_CHUNKS = 4


def row_factors(ratios, pair_row, lengths):
    seq_count = ratios.shape[0]
    seq_slots = jnp.arange(seq_count, dtype=jnp.int32)
    chosen = pair_row[0::2]
    rejected = pair_row[1::2]
    pick_chosen = (chosen[:, None] == seq_slots[None, :]).astype(jnp.float32)
    pick_rejected = (rejected[:, None] == seq_slots[None, :]).astype(jnp.float32)
    margin = beta_dpo * (
        jnp.sum(pick_chosen * ratios[None, :], axis=1)
        - jnp.sum(pick_rejected * ratios[None, :], axis=1)
    )
    weight = beta_dpo * jax.nn.sigmoid(-margin)
    coefficient = jnp.sum(weight[:, None] * (pick_rejected - pick_chosen), axis=0)
    position = jnp.arange(LEN, dtype=jnp.int32)
    in_length = (position[None, :] < lengths[:, None]).astype(jnp.float32)
    return coefficient[:, None] * in_length


def scale_rows(out_grad, log_ratio, pair_order, seq_len):
    factors = row_factors(log_ratio, pair_order[0], seq_len)
    return (out_grad.astype(jnp.float32) * factors.reshape(-1)[:, None]).astype(jnp.bfloat16)


def adam(grad, master, moment, second):
    new_moment = beta_one * moment + (1.0 - beta_one) * grad
    new_second = beta_two * second + (1.0 - beta_two) * grad * grad
    update = (new_moment * (1.0 / bias_one)) / (
        jnp.sqrt(new_second * (1.0 / bias_two)) + adam_eps
    )
    new_master = master - rate_learn * update
    return new_master, new_moment, new_second, update


def body_general(
    out_grad, hidden_act, log_ratio, pair_order, seq_len, master, moment, second, next_act
):
    scaled = scale_rows(out_grad, log_ratio, pair_order, seq_len)
    mine = lax.all_to_all(scaled, "dp", split_axis=1, concat_axis=0, tiled=True)
    hidden = lax.all_gather(hidden_act, "dp", axis=0, tiled=True)
    grad = lax.dot_general(
        mine, hidden, (((0,), (0,)), ((), ())), preferred_element_type=jnp.float32
    )
    new_master, new_moment, new_second, update = adam(grad, master, moment, second)
    weights = lax.all_gather(new_master.astype(jnp.bfloat16), "dp", axis=0, tiled=True)
    partial_next = lax.dot_general(
        next_act, weights, (((1,), (1,)), ((), ())), preferred_element_type=jnp.float32
    )
    summed = lax.psum_scatter(
        partial_next.astype(jnp.bfloat16), "tensor", scatter_dimension=1, tiled=True
    )
    return (new_master, new_moment, new_second, update, summed)


def planes(pairs):
    return [(2 * a + core, 2 * b + core) for a, b in pairs for core in (0, 1)]


PAIR = planes([(0, 1), (1, 0), (2, 3), (3, 2)])
MIDDLE = planes([(1, 2), (2, 1)])
OUTWARD = planes([(1, 0), (2, 3)])
INWARD = planes([(0, 1), (3, 2)])
CORES = [(2 * z + core, 2 * z + 1 - core) for z in range(4) for core in (0, 1)]


def step_kernel(n_act, has_prior, *refs):
    scaled_ref = refs[0]
    acts = refs[1 : 1 + n_act]
    master_ref, moment_ref, second_ref = refs[1 + n_act : 4 + n_act]
    outs = refs[4 + n_act + (4 if has_prior else 0) :]
    tokens = acts[0].shape[0]
    grad = None
    for i, act in enumerate(acts):
        term = jnp.dot(
            scaled_ref[:, i * tokens : (i + 1) * tokens],
            act[...],
            preferred_element_type=jnp.float32,
        )
        grad = term if grad is None else grad + term
    new_master, new_moment, new_second, update = adam(
        grad, master_ref[...], moment_ref[...], second_ref[...]
    )
    outs[0][...] = new_master
    outs[1][...] = new_moment
    outs[2][...] = new_second
    outs[3][...] = update
    outs[4][...] = new_master.astype(jnp.bfloat16)


def step_rows(r, scaled_t, acts, master, moment, second, prior):
    rows_all, cols = master.shape
    rows = rows_all // ROW_CHUNKS
    tokens = acts[0].shape[0]
    tile = 768
    state = pl.BlockSpec((rows, tile), lambda t: (r, t))
    in_specs = (
        [pl.BlockSpec((rows, scaled_t.shape[1]), lambda t: (r, 0))]
        + [pl.BlockSpec((tokens, tile), lambda t: (0, t))] * len(acts)
        + [state] * 3
    )
    operands = [scaled_t, *acts, master, moment, second]
    aliases = {}
    if prior is not None:
        for i, array in enumerate(prior):
            aliases[len(operands)] = i
            operands.append(array)
            in_specs.append(pl.BlockSpec(memory_space=pl.ANY))
    full = jax.ShapeDtypeStruct((rows_all, cols), jnp.float32)
    outs = pl.pallas_call(
        functools.partial(step_kernel, len(acts), prior is not None),
        grid=(cols // tile,),
        in_specs=in_specs,
        out_specs=[state] * 4 + [pl.BlockSpec((rows, tile), lambda t: (0, t))],
        out_shape=[full] * 4 + [jax.ShapeDtypeStruct((rows, cols), jnp.bfloat16)],
        input_output_aliases=aliases,
        compiler_params=pltpu.CompilerParams(vmem_limit_bytes=48 * 1024 * 1024),
        cost_estimate=pl.CostEstimate(
            flops=2 * rows * cols * tokens * len(acts),
            bytes_accessed=2 * tokens * len(acts) * cols + 30 * rows * cols,
            transcendentals=rows * cols,
        ),
        name="gradient_adam",
    )(*operands)
    return outs[:4], outs[4]


def times(tokens, rows):
    return lax.dot_general(
        tokens, rows, (((1,), (1,)), ((), ())), preferred_element_type=jnp.float32
    ).astype(jnp.bfloat16)


def by_plane(parts, z):
    odd, high = (z & 1) == 1, (z & 2) == 2
    a = [jnp.where(odd, parts[i ^ 1], parts[i]) for i in range(4)]
    return [jnp.where(high, a[i ^ 2], a[i]) for i in range(4)]


def body_planes(
    out_grad, hidden_act, log_ratio, pair_order, seq_len, master, moment, second, next_act
):
    send = lambda array, pairs: lax.ppermute(array, "dp", pairs)
    k = lax.axis_index("dp")
    j = lax.axis_index("tensor")
    z, core = k // 2, k % 2
    inner = (z == 1) | (z == 2)
    tokens = hidden_act.shape[0]
    model = out_grad.shape[1]
    rows_all, cols = master.shape

    pair_act = send(hidden_act, PAIR)
    middle_act = send(hidden_act, MIDDLE)
    forward_act = send(pair_act, MIDDLE)
    far_one = send(middle_act, OUTWARD)
    far_two = send(forward_act, OUTWARD)
    third = jnp.where(inner, middle_act, far_one)
    fourth = jnp.where(inner, forward_act, far_two)
    acts = []
    for act in (hidden_act, pair_act, third, fourth):
        acts += [act, send(act, CORES)]

    scaled = scale_rows(out_grad, log_ratio, pair_order, seq_len)
    share = tokens // 4
    part = lax.dynamic_slice_in_dim(scaled, j * share, share, 0)
    part = lax.all_to_all(
        part.reshape(share, 8, model // 8), "dp", split_axis=1, concat_axis=0, tiled=False
    )
    whole = lax.all_gather(part, "tensor", axis=0, tiled=False)
    order = jnp.array(
        [[0, 1, 2, 3], [1, 0, 2, 3], [2, 3, 1, 0], [3, 2, 1, 0]], dtype=jnp.int32
    )[z]
    order = jnp.stack([order * 2 + core, order * 2 + 1 - core], axis=1).reshape(8)
    whole = jnp.take(whole, order, axis=1)
    scaled_t = whole.transpose(3, 1, 0, 2).reshape(model // 8, 8 * tokens)

    next_two = jnp.concatenate([next_act, send(next_act, CORES)], axis=0)
    next_pair = send(next_act, INWARD)
    next_pair = jnp.concatenate([next_pair, send(next_pair, CORES)], axis=0)

    rows = rows_all // ROW_CHUNKS
    prior = None
    sums = []
    for r in range(ROW_CHUNKS):
        prior, own = step_rows(r, scaled_t, acts, master, moment, second, prior)
        pair = send(own, PAIR)
        middle = send(own, MIDDLE)
        forward = send(pair, MIDDLE)
        product = [times(next_two, block) for block in (own, pair, forward, middle)]
        zero = jnp.zeros_like(product[0])
        other = [zero, zero] + [times(next_pair, block) for block in (forward, middle)]
        stack = []
        for a, b in zip(by_plane(product, z), by_plane(other, z)):
            stack += [a, b]
        total = lax.psum_scatter(
            jnp.concatenate(stack, axis=0), "tensor", scatter_dimension=0, tiled=True
        )
        count = next_two.shape[0]
        sums.append(total[:count] + send(total[count:], OUTWARD))
    columns = jnp.concatenate(sums, axis=1)
    half = columns.shape[0] // 2
    mine, theirs = columns[:half], send(columns[half:], CORES)
    next_out = jnp.concatenate(
        [jnp.where(core == 0, mine, theirs), jnp.where(core == 0, theirs, mine)], axis=1
    )
    return (*prior, next_out)


def solution(mesh):
    fits = mesh.shape["dp"] == 8 and mesh.shape["tensor"] == 4
    return jax.shard_map(
        body_planes if fits else body_general,
        mesh=mesh,
        in_specs=(
            P("dp", None),
            P("dp", "tensor"),
            P("dp"),
            P("dp", None),
            P("dp"),
            P("dp", "tensor"),
            P("dp", "tensor"),
            P("dp", "tensor"),
            P("dp", "tensor"),
        ),
        out_specs=(
            P("dp", "tensor"),
            P("dp", "tensor"),
            P("dp", "tensor"),
            P("dp", "tensor"),
            P("dp", "tensor"),
        ),
        check_vma=False,
    )
```

```python
import functools

import jax
import jax.numpy as jnp
from jax import lax
from jax.experimental import pallas as pl
from jax.experimental.pallas import tpu as pltpu
from jax.sharding import PartitionSpec as P

LEN = 32


beta_dpo = 0.1
beta_one = 0.9
beta_two = 0.999
bias_one = 1.0 - 0.9**10
bias_two = 1.0 - 0.999**10
adam_eps = 1e-08
rate_learn = 0.001

ROW_CHUNKS = 2


def row_factors(ratios, pair_row, lengths):
    seq_count = ratios.shape[0]
    seq_slots = jnp.arange(seq_count, dtype=jnp.int32)
    chosen = pair_row[0::2]
    rejected = pair_row[1::2]
    pick_chosen = (chosen[:, None] == seq_slots[None, :]).astype(jnp.float32)
    pick_rejected = (rejected[:, None] == seq_slots[None, :]).astype(jnp.float32)
    margin = beta_dpo * (
        jnp.sum(pick_chosen * ratios[None, :], axis=1)
        - jnp.sum(pick_rejected * ratios[None, :], axis=1)
    )
    weight = beta_dpo * jax.nn.sigmoid(-margin)
    coefficient = jnp.sum(weight[:, None] * (pick_rejected - pick_chosen), axis=0)
    position = jnp.arange(LEN, dtype=jnp.int32)
    in_length = (position[None, :] < lengths[:, None]).astype(jnp.float32)
    return coefficient[:, None] * in_length


def scale_rows(out_grad, log_ratio, pair_order, seq_len):
    factors = row_factors(log_ratio, pair_order[0], seq_len)
    return (out_grad.astype(jnp.float32) * factors.reshape(-1)[:, None]).astype(jnp.bfloat16)


def adam(grad, master, moment, second):
    new_moment = beta_one * moment + (1.0 - beta_one) * grad
    new_second = beta_two * second + (1.0 - beta_two) * grad * grad
    update = (new_moment * (1.0 / bias_one)) / (
        jnp.sqrt(new_second * (1.0 / bias_two)) + adam_eps
    )
    new_master = master - rate_learn * update
    return new_master, new_moment, new_second, update


def body_general(
    out_grad, hidden_act, log_ratio, pair_order, seq_len, master, moment, second, next_act
):
    scaled = scale_rows(out_grad, log_ratio, pair_order, seq_len)
    mine = lax.all_to_all(scaled, "dp", split_axis=1, concat_axis=0, tiled=True)
    hidden = lax.all_gather(hidden_act, "dp", axis=0, tiled=True)
    grad = lax.dot_general(
        mine, hidden, (((0,), (0,)), ((), ())), preferred_element_type=jnp.float32
    )
    new_master, new_moment, new_second, update = adam(grad, master, moment, second)
    weights = lax.all_gather(new_master.astype(jnp.bfloat16), "dp", axis=0, tiled=True)
    partial_next = lax.dot_general(
        next_act, weights, (((1,), (1,)), ((), ())), preferred_element_type=jnp.float32
    )
    summed = lax.psum_scatter(
        partial_next.astype(jnp.bfloat16), "tensor", scatter_dimension=1, tiled=True
    )
    return (new_master, new_moment, new_second, update, summed)


def planes(pairs):
    return [(2 * a + core, 2 * b + core) for a, b in pairs for core in (0, 1)]


PAIR = planes([(0, 1), (1, 0), (2, 3), (3, 2)])
MIDDLE = planes([(1, 2), (2, 1)])
OUTWARD = planes([(1, 0), (2, 3)])
INWARD = planes([(0, 1), (3, 2)])


def homeward(pairs, core):
    return [
        ((2 * a + core) * 4 + 2 * y + x, (2 * b + y) * 4 + 2 * (a // 2) + x)
        for a, b in pairs
        for y in (0, 1)
        for x in (0, 1)
    ]


CORES = [(2 * z + core, 2 * z + 1 - core) for z in range(4) for core in (0, 1)]


def step_kernel(n_act, skip, *refs):
    scaled_ref = refs[0]
    acts = refs[1 : 1 + n_act]
    master_ref, moment_ref, second_ref = refs[1 + n_act : 4 + n_act]
    outs = refs[4 + n_act + skip :]
    tokens = acts[0].shape[0]
    grad = None
    for i, act in enumerate(acts):
        term = jnp.dot(
            scaled_ref[:, i * tokens : (i + 1) * tokens],
            act[...],
            preferred_element_type=jnp.float32,
        )
        grad = term if grad is None else grad + term
    new_master, new_moment, new_second, update = adam(
        grad, master_ref[...], moment_ref[...], second_ref[...]
    )
    outs[0][...] = new_master
    outs[1][...] = new_moment
    outs[2][...] = new_second
    outs[3][...] = update
    outs[4][...] = new_master.astype(jnp.bfloat16)


def step_rows(r, scaled_t, acts, master, moment, second, prior, behind):
    rows_all, cols = master.shape
    rows = rows_all // ROW_CHUNKS
    tokens = acts[0].shape[0]
    tile = 768
    state = pl.BlockSpec((rows, tile), lambda t: (r, t))
    in_specs = (
        [pl.BlockSpec((rows, scaled_t.shape[1]), lambda t: (r, 0))]
        + [pl.BlockSpec((tokens, tile), lambda t: (0, t))] * len(acts)
        + [state] * 3
    )
    operands = [scaled_t, *acts, master, moment, second]
    aliases = {}
    if prior is not None:
        for i, array in enumerate(prior):
            aliases[len(operands)] = i
            operands.append(array)
            in_specs.append(pl.BlockSpec(memory_space=pl.ANY))
    for array in behind:
        operands.append(array)
        in_specs.append(pl.BlockSpec(memory_space=pl.ANY))
    full = jax.ShapeDtypeStruct((rows_all, cols), jnp.float32)
    outs = pl.pallas_call(
        functools.partial(step_kernel, len(acts), len(operands) - 4 - len(acts)),
        grid=(cols // tile,),
        in_specs=in_specs,
        out_specs=[state] * 4 + [pl.BlockSpec((rows, tile), lambda t: (0, t))],
        out_shape=[full] * 4 + [jax.ShapeDtypeStruct((rows, cols), jnp.bfloat16)],
        input_output_aliases=aliases,
        compiler_params=pltpu.CompilerParams(vmem_limit_bytes=60 * 1024 * 1024),
        cost_estimate=SMALL,
        name="gradient_adam",
    )(*operands)
    return outs[:4], outs[4]


SMALL = pl.CostEstimate(flops=1000, bytes_accessed=1000, transcendentals=0)


def times(tokens, rows):
    return lax.dot_general(
        tokens, rows, (((1,), (1,)), ((), ())), preferred_element_type=jnp.float32
    ).astype(jnp.bfloat16)


def product_kernel(x_first, n_weights, tiles, place_ref, mine_ref, other_ref, *refs):
    weights = refs[:n_weights]
    out_ref, all_ref = refs[-2:]
    rows = weights[0].shape[0]
    step = pl.program_id(0)

    @pl.when(step == 0)
    def _():
        for i, ref in enumerate(weights):
            all_ref[i * rows : (i + 1) * rows] = ref[...]

    def store(tokens_ref):
        out = times(tokens_ref[...], all_ref[...])
        give = place_ref[0]
        half = out.shape[1] // 2
        for at, block in ((give, out[:, :half]), (1 - give, out[:, half:])):
            if x_first:
                out_ref[at, 0] = block
            else:
                out_ref[0, at] = block

    pl.when(step < tiles)(functools.partial(store, mine_ref))
    pl.when(step >= tiles)(functools.partial(store, other_ref))


def products(place, x_first, tokens, weights, behind=()):
    count, cols = tokens[0].shape
    rows = weights[0].shape[0]
    features = rows * len(weights) // 2
    tile = 256
    tiles = count // tile

    def out_map(t, place):
        y = jnp.where(t < tiles, place[1], 1 - place[1])
        return (0, y, t % tiles, 0) if x_first else (y, 0, t % tiles, 0)

    in_specs = [
        pl.BlockSpec((tile, cols), lambda t, place: (jnp.minimum(t, tiles - 1), 0)),
        pl.BlockSpec((tile, cols), lambda t, place: (jnp.maximum(t - tiles, 0), 0)),
    ]
    in_specs += [pl.BlockSpec((rows, cols), lambda t, place: (0, 0))] * len(weights)
    in_specs += [pl.BlockSpec(memory_space=pl.ANY)] * len(behind)
    return pl.pallas_call(
        functools.partial(product_kernel, x_first, len(weights), tiles),
        grid_spec=pltpu.PrefetchScalarGridSpec(
            num_scalar_prefetch=1,
            grid=(2 * tiles,),
            in_specs=in_specs,
            out_specs=pl.BlockSpec(
                (2, 1, tile, features) if x_first else (1, 2, tile, features), out_map
            ),
            scratch_shapes=[pltpu.VMEM((rows * len(weights), cols), jnp.bfloat16)],
        ),
        out_shape=jax.ShapeDtypeStruct((2, 2, count, features), jnp.bfloat16),
        compiler_params=pltpu.CompilerParams(vmem_limit_bytes=60 * 1024 * 1024),
        cost_estimate=SMALL,
        name="product",
    )(place, *tokens, *weights, *behind)


def add_up(stack, x_first, behind=None):
    for step in ((1, 2) if x_first else (2, 1)):
        given = lax.ppermute(stack[1], "tensor", [(i, i ^ step) for i in range(4)])
        if behind is not None:
            given, behind = lax.optimization_barrier((given, behind))
        stack = (stack[0].astype(jnp.float32) + given.astype(jnp.float32)).astype(jnp.bfloat16)
    return stack


def body_planes(
    out_grad, hidden_act, log_ratio, pair_order, seq_len, master, moment, second, next_act
):
    send = lambda array, pairs: lax.ppermute(array, "dp", pairs)
    after = lax.optimization_barrier
    send_all = lambda array, pairs: lax.ppermute(array, ("dp", "tensor"), pairs)
    k = lax.axis_index("dp")
    j = lax.axis_index("tensor")
    z, core = k // 2, k % 2
    inner = (z == 1) | (z == 2)
    tokens = hidden_act.shape[0]
    model = out_grad.shape[1]
    rows_all, cols = master.shape

    pair_act = send(hidden_act, PAIR)
    middle_act = send(hidden_act, MIDDLE)

    scaled = scale_rows(out_grad, log_ratio, pair_order, seq_len)
    share = tokens // 4
    width = model // 4
    part = lax.dynamic_slice_in_dim(scaled, j * share, share, 0)
    pieces = [lax.dynamic_slice_in_dim(part, (z ^ d) * width, width, 1) for d in range(4)]
    for d in (1, 2, 3):
        pieces[d] = send(pieces[d], planes([(p, p ^ d) for p in range(4)]))

    pair_act, middle_act, own_act, own_next, pieces = after(
        (pair_act, middle_act, hidden_act, next_act, pieces)
    )
    forward_act = send(pair_act, MIDDLE)
    far_one = send(middle_act, OUTWARD)
    rows = next_act.shape[0] // 2
    next_inward = [send(own_next[:rows], INWARD), send(own_next[rows:], INWARD)]
    pieces = [
        pieces[0],
        pieces[1],
        jnp.where(inner, pieces[3], pieces[2]),
        jnp.where(inner, pieces[2], pieces[3]),
    ]
    pieces = jnp.stack(pieces)
    half = width // 2
    keep = lax.dynamic_slice_in_dim(pieces, core * half, half, 2)
    give = lax.dynamic_slice_in_dim(pieces, (1 - core) * half, half, 2)
    part = jnp.stack([keep, send(give, CORES)], axis=1).reshape(1, 8, share, half)
    x, y = j % 2, j // 2
    given = lax.ppermute(part, "tensor", [(i, i ^ 1) for i in range(4)])
    part = jnp.concatenate([jnp.where(x == 0, part, given), jnp.where(x == 0, given, part)], 0)
    given = lax.ppermute(part, "tensor", [(i, i ^ 2) for i in range(4)])
    own_swap = send(own_act, CORES)
    pair_act, own_swap = after((pair_act, own_swap))
    pair_swap = send(pair_act, CORES)

    forward_act, far_one, middle_act, own_next, pair_swap, part, next_inward[0] = after(
        (forward_act, far_one, middle_act, own_next, pair_swap, part, next_inward[0])
    )
    far_two = send(forward_act, OUTWARD)
    next_middle = send(own_next, MIDDLE)
    whole = jnp.concatenate([jnp.where(y == 0, part, given), jnp.where(y == 0, given, part)], 0)
    scaled_t = whole.transpose(3, 1, 0, 2).reshape(half, 8 * tokens)
    third = jnp.where(inner, middle_act, far_one)
    third_swap = send(third, CORES)
    own_next, third_swap = after((own_next, third_swap))
    next_own = [next_act, send(own_next, CORES)]
    fourth = jnp.where(inner, forward_act, far_two)
    fourth_swap = send(fourth, CORES)
    acts = [hidden_act, own_swap, pair_act, pair_swap, third, third_swap, fourth, fourth_swap]

    behind = [next_own[1], next_inward[1]]
    prior, own_one = step_rows(0, scaled_t, acts, master, moment, second, None, behind)
    pair_one = send(own_one, PAIR)
    next_inward, _ = after((next_inward, own_one))
    next_far = [send(array, MIDDLE) for array in next_inward]
    prior, own_two = step_rows(1, scaled_t, acts, master, moment, second, prior, [next_middle])
    pair_two = send(own_two, PAIR)

    place = jnp.stack([(z & 1) ^ x, core ^ y])
    next_middle, _ = after((next_middle, own_two))
    next_middle = [next_middle, send(next_middle, CORES)]
    one, two = (own_one, pair_one), (own_two, pair_two)
    near_one = products(place, True, next_own, one)
    middle_one = products(place, False, next_middle, one, [near_one])
    near_two = products(place, True, next_own, two, [middle_one])
    middle_two = products(place, False, next_middle, two, [near_two])
    next_far, _ = after((next_far, own_two))
    next_far = [[array, send(array, CORES)] for array in next_far]
    both = (own_one, own_two, pair_one, pair_two)
    far_one = products(place, True, next_far[0], both, [middle_two])
    far_two = products(place, False, next_far[1], both, [far_one])
    near = [add_up(near_one, True, middle_one), add_up(near_two, True, middle_two)]
    middle = [add_up(middle_one, False), add_up(middle_two, False, far_one)]
    far = [add_up(far_one, True, far_two), add_up(far_two, False)]
    near, middle = jnp.concatenate(near, axis=1), jnp.concatenate(middle, axis=1)
    far = jnp.concatenate(far, axis=0)

    parts = []
    for side in (0, 1):
        parts.append(
            send_all(near, homeward([(p, p) for p in range(4)], side))
            + send_all(middle, homeward([(1, 2), (2, 1)], side))
            + send_all(far, homeward([(1, 3), (2, 0)], side))
        )
    return (*prior, jnp.concatenate(parts, axis=1))


def solution(mesh):
    fits = mesh.shape["dp"] == 8 and mesh.shape["tensor"] == 4
    return jax.shard_map(
        body_planes if fits else body_general,
        mesh=mesh,
        in_specs=(
            P("dp", None),
            P("dp", "tensor"),
            P("dp"),
            P("dp", None),
            P("dp"),
            P("dp", "tensor"),
            P("dp", "tensor"),
            P("dp", "tensor"),
            P("dp", "tensor"),
        ),
        out_specs=(
            P("dp", "tensor"),
            P("dp", "tensor"),
            P("dp", "tensor"),
            P("dp", "tensor"),
            P("dp", "tensor"),
        ),
        check_vma=False,
    )
```

```python
import functools

import jax
import jax.numpy as jnp
from jax import lax
from jax.experimental import pallas as pl
from jax.experimental.pallas import tpu as pltpu
from jax.sharding import PartitionSpec as P

LEN = 32


beta_dpo = 0.1
beta_one = 0.9
beta_two = 0.999
bias_one = 1.0 - 0.9**10
bias_two = 1.0 - 0.999**10
adam_eps = 1e-08
rate_learn = 0.001

ROW_PARTS = ((0, 2), (2, 2), (4, 4))


def row_factors(ratios, pair_row, lengths):
    seq_count = ratios.shape[0]
    seq_slots = jnp.arange(seq_count, dtype=jnp.int32)
    chosen = pair_row[0::2]
    rejected = pair_row[1::2]
    pick_chosen = (chosen[:, None] == seq_slots[None, :]).astype(jnp.float32)
    pick_rejected = (rejected[:, None] == seq_slots[None, :]).astype(jnp.float32)
    margin = beta_dpo * (
        jnp.sum(pick_chosen * ratios[None, :], axis=1)
        - jnp.sum(pick_rejected * ratios[None, :], axis=1)
    )
    weight = beta_dpo * jax.nn.sigmoid(-margin)
    coefficient = jnp.sum(weight[:, None] * (pick_rejected - pick_chosen), axis=0)
    position = jnp.arange(LEN, dtype=jnp.int32)
    in_length = (position[None, :] < lengths[:, None]).astype(jnp.float32)
    return coefficient[:, None] * in_length


def scale_rows(out_grad, log_ratio, pair_order, seq_len):
    factors = row_factors(log_ratio, pair_order[0], seq_len)
    return (out_grad.astype(jnp.float32) * factors.reshape(-1)[:, None]).astype(jnp.bfloat16)


def adam(grad, master, moment, second):
    new_moment = beta_one * moment + (1.0 - beta_one) * grad
    new_second = beta_two * second + (1.0 - beta_two) * grad * grad
    update = (new_moment * (1.0 / bias_one)) / (
        jnp.sqrt(new_second * (1.0 / bias_two)) + adam_eps
    )
    new_master = master - rate_learn * update
    return new_master, new_moment, new_second, update


def body_general(
    out_grad, hidden_act, log_ratio, pair_order, seq_len, master, moment, second, next_act
):
    scaled = scale_rows(out_grad, log_ratio, pair_order, seq_len)
    mine = lax.all_to_all(scaled, "dp", split_axis=1, concat_axis=0, tiled=True)
    hidden = lax.all_gather(hidden_act, "dp", axis=0, tiled=True)
    grad = lax.dot_general(
        mine, hidden, (((0,), (0,)), ((), ())), preferred_element_type=jnp.float32
    )
    new_master, new_moment, new_second, update = adam(grad, master, moment, second)
    weights = lax.all_gather(new_master.astype(jnp.bfloat16), "dp", axis=0, tiled=True)
    partial_next = lax.dot_general(
        next_act, weights, (((1,), (1,)), ((), ())), preferred_element_type=jnp.float32
    )
    summed = lax.psum_scatter(
        partial_next.astype(jnp.bfloat16), "tensor", scatter_dimension=1, tiled=True
    )
    return (new_master, new_moment, new_second, update, summed)


def planes(pairs):
    return [(2 * a + core, 2 * b + core) for a, b in pairs for core in (0, 1)]


PAIR = planes([(0, 1), (1, 0), (2, 3), (3, 2)])
MIDDLE = planes([(1, 2), (2, 1)])
OUTWARD = planes([(1, 0), (2, 3)])
INWARD = planes([(0, 1), (3, 2)])


def homeward(pairs, core, flip=0):
    return [
        ((2 * a + core) * 4 + 2 * y + x, (2 * b + (y ^ flip)) * 4 + 2 * (a // 2) + x)
        for a, b in pairs
        for y in (0, 1)
        for x in (0, 1)
    ]


CORES = [(2 * z + core, 2 * z + 1 - core) for z in range(4) for core in (0, 1)]


def step_kernel(n_act, skip, *refs):
    scaled_ref = refs[0]
    acts = refs[1 : 1 + n_act]
    master_ref, moment_ref, second_ref = refs[1 + n_act : 4 + n_act]
    outs = refs[4 + n_act + skip :]
    tokens = acts[0].shape[0]
    grad = None
    for i, act in enumerate(acts):
        term = jnp.dot(
            scaled_ref[:, i * tokens : (i + 1) * tokens],
            act[...],
            preferred_element_type=jnp.float32,
        )
        grad = term if grad is None else grad + term
    new_master, new_moment, new_second, update = adam(
        grad, master_ref[...], moment_ref[...], second_ref[...]
    )
    outs[0][...] = new_master
    outs[1][...] = new_moment
    outs[2][...] = new_second
    outs[3][...] = update
    outs[4][...] = new_master.astype(jnp.bfloat16)


def step_rows(part, scaled_t, acts, master, moment, second, prior, behind):
    rows_all, cols = master.shape
    rows = rows_all // 8 * part[1]
    r = part[0] // part[1]
    tokens = acts[0].shape[0]
    tile = 768
    state = pl.BlockSpec((rows, tile), lambda t: (r, t))
    in_specs = (
        [pl.BlockSpec((rows, scaled_t.shape[1]), lambda t: (r, 0))]
        + [pl.BlockSpec((tokens, tile), lambda t: (0, t))] * len(acts)
        + [state] * 3
    )
    operands = [scaled_t, *acts, master, moment, second]
    aliases = {}
    if prior is not None:
        for i, array in enumerate(prior):
            aliases[len(operands)] = i
            operands.append(array)
            in_specs.append(pl.BlockSpec(memory_space=pl.ANY))
    for array in behind:
        operands.append(array)
        in_specs.append(pl.BlockSpec(memory_space=pl.ANY))
    full = jax.ShapeDtypeStruct((rows_all, cols), jnp.float32)
    outs = pl.pallas_call(
        functools.partial(step_kernel, len(acts), len(operands) - 4 - len(acts)),
        grid=(cols // tile,),
        in_specs=in_specs,
        out_specs=[state] * 4 + [pl.BlockSpec((rows, tile), lambda t: (0, t))],
        out_shape=[full] * 4 + [jax.ShapeDtypeStruct((rows, cols), jnp.bfloat16)],
        input_output_aliases=aliases,
        compiler_params=pltpu.CompilerParams(vmem_limit_bytes=60 * 1024 * 1024),
        cost_estimate=SMALL,
        name="gradient_adam",
    )(*operands)
    return outs[:4], outs[4]


SMALL = pl.CostEstimate(flops=1000, bytes_accessed=1000, transcendentals=0)


def times(tokens, rows):
    return lax.dot_general(
        tokens, rows, (((1,), (1,)), ((), ())), preferred_element_type=jnp.float32
    ).astype(jnp.bfloat16)


def product_kernel(x_first, n_weights, tiles, place_ref, mine_ref, other_ref, *refs):
    weights = refs[:n_weights]
    out_ref, all_ref = refs[-2:]
    step = pl.program_id(0)

    @pl.when(step == 0)
    def _():
        first = 0
        for ref in weights:
            rows = ref.shape[0]
            all_ref[first : first + rows] = ref[...]
            first += rows

    def store(tokens_ref):
        out = times(tokens_ref[...], all_ref[...])
        give = place_ref[0]
        half = out.shape[1] // 2
        for at, block in ((give, out[:, :half]), (1 - give, out[:, half:])):
            if x_first:
                out_ref[at, 0] = block
            else:
                out_ref[0, at] = block

    pl.when(step < tiles)(functools.partial(store, mine_ref))
    pl.when(step >= tiles)(functools.partial(store, other_ref))


def products(place, x_first, tokens, weights, behind=()):
    count, cols = tokens[0].shape
    features = sum(block.shape[0] for block in weights) // 2
    tile = 256
    tiles = count // tile

    def out_map(t, place):
        y = jnp.where(t < tiles, place[1], 1 - place[1])
        return (0, y, t % tiles, 0) if x_first else (y, 0, t % tiles, 0)

    in_specs = [
        pl.BlockSpec((tile, cols), lambda t, place: (jnp.minimum(t, tiles - 1), 0)),
        pl.BlockSpec((tile, cols), lambda t, place: (jnp.maximum(t - tiles, 0), 0)),
    ]
    in_specs += [pl.BlockSpec(block.shape, lambda t, place: (0, 0)) for block in weights]
    in_specs += [pl.BlockSpec(memory_space=pl.ANY)] * len(behind)
    return pl.pallas_call(
        functools.partial(product_kernel, x_first, len(weights), tiles),
        grid_spec=pltpu.PrefetchScalarGridSpec(
            num_scalar_prefetch=1,
            grid=(2 * tiles,),
            in_specs=in_specs,
            out_specs=pl.BlockSpec(
                (2, 1, tile, features) if x_first else (1, 2, tile, features), out_map
            ),
            scratch_shapes=[pltpu.VMEM((2 * features, cols), jnp.bfloat16)],
        ),
        out_shape=jax.ShapeDtypeStruct((2, 2, count, features), jnp.bfloat16),
        compiler_params=pltpu.CompilerParams(vmem_limit_bytes=60 * 1024 * 1024),
        cost_estimate=SMALL,
        name="product",
    )(place, *tokens, *weights, *behind)


def add_step(stack, step):
    given = lax.ppermute(stack[1], "tensor", [(i, i ^ step) for i in range(4)])
    return (stack[0].astype(jnp.float32) + given.astype(jnp.float32)).astype(jnp.bfloat16)


def body_planes(
    out_grad, hidden_act, log_ratio, pair_order, seq_len, master, moment, second, next_act
):
    send = lambda array, pairs: lax.ppermute(array, "dp", pairs)
    after = lax.optimization_barrier
    send_all = lambda array, pairs: lax.ppermute(array, ("dp", "tensor"), pairs)
    k = lax.axis_index("dp")
    j = lax.axis_index("tensor")
    z, core = k // 2, k % 2
    inner = (z == 1) | (z == 2)
    tokens = hidden_act.shape[0]
    model = out_grad.shape[1]
    rows_all, cols = master.shape

    pair_act = send(hidden_act, PAIR)
    middle_act = send(hidden_act, MIDDLE)

    scaled = scale_rows(out_grad, log_ratio, pair_order, seq_len)
    share = tokens // 4
    width = model // 4
    part = lax.dynamic_slice_in_dim(scaled, j * share, share, 0)
    pieces = [lax.dynamic_slice_in_dim(part, (z ^ d) * width, width, 1) for d in range(4)]
    for d in (1, 2, 3):
        pieces[d] = send(pieces[d], planes([(p, p ^ d) for p in range(4)]))

    rows = next_act.shape[0] // 2
    next_parts = [next_act[:rows], next_act[rows:]]
    pair_act, middle_act, own_act, own_next, next_parts, pieces = after(
        (pair_act, middle_act, hidden_act, next_act, next_parts, pieces)
    )
    forward_act = send(pair_act, MIDDLE)
    far_one = send(middle_act, OUTWARD)
    next_inward = send(own_next, INWARD)
    pieces = [
        pieces[0],
        pieces[1],
        jnp.where(inner, pieces[3], pieces[2]),
        jnp.where(inner, pieces[2], pieces[3]),
    ]
    pieces = jnp.stack(pieces)
    half = width // 2
    keep = lax.dynamic_slice_in_dim(pieces, core * half, half, 2)
    give = lax.dynamic_slice_in_dim(pieces, (1 - core) * half, half, 2)
    part = jnp.stack([keep, send(give, CORES)], axis=1).reshape(1, 8, share, half)
    x, y = j % 2, j // 2
    given = lax.ppermute(part, "tensor", [(i, i ^ 1) for i in range(4)])
    part = jnp.concatenate([jnp.where(x == 0, part, given), jnp.where(x == 0, given, part)], 0)
    given = lax.ppermute(part, "tensor", [(i, i ^ 2) for i in range(4)])
    own_swap = send(own_act, CORES)
    pair_act, own_swap = after((pair_act, own_swap))
    pair_swap = send(pair_act, CORES)

    forward_act, far_one, middle_act, own_next, next_parts, pair_swap, part = after(
        (forward_act, far_one, middle_act, own_next, next_parts, pair_swap, part)
    )
    far_two = send(forward_act, OUTWARD)
    next_middle = [send(array, MIDDLE) for array in next_parts]
    third = jnp.where(inner, middle_act, far_one)
    third, given = after((third, given))
    third_swap = send(third, CORES)
    whole = jnp.concatenate([jnp.where(y == 0, part, given), jnp.where(y == 0, given, part)], 0)
    scaled_t = whole.transpose(3, 1, 0, 2).reshape(half, 8 * tokens)
    own_next, third_swap = after((own_next, third_swap))
    next_own = [next_act, send(own_next, CORES)]
    far_two, next_middle[0], scaled_t = after((far_two, next_middle[0], scaled_t))
    fourth = jnp.where(inner, forward_act, far_two)
    fourth_swap = send(fourth, CORES)
    acts = [hidden_act, own_swap, pair_act, pair_swap, third, third_swap, fourth, fourth_swap]

    next_far = send(next_inward, MIDDLE)

    place = jnp.stack([(z & 1) ^ x, core ^ y])
    prior, owns, pairs = None, [], []
    for part in ROW_PARTS:
        behind = pairs[:1] if len(owns) == 2 else [next_own[1], next_inward]
        prior, own = step_rows(part, scaled_t, acts, master, moment, second, prior, behind)
        owns.append(own)
        pairs.append(send(own, PAIR))
    one, two = tuple(owns[:2] + pairs[:2]), (owns[2], pairs[2])
    both = tuple(owns + pairs)

    def swapped(array, behind):
        array, _ = after((array, behind))
        return [array, send(array, CORES)]

    near_one = products(place, True, next_own, one, owns[2:])
    next_far = swapped(next_far, near_one)
    far_one = products(place, False, next_far, one, [near_one])
    near_two = products(place, True, next_own, two, [far_one])
    near_one, far_one = add_step(add_step(near_one, 1), 2), add_step(add_step(far_one, 2), 1)
    far_two = products(place, False, next_far, two, [near_two])
    next_middle[0] = swapped(next_middle[0], near_one)
    next_middle[1] = swapped(next_middle[1], near_two)
    middle_one = products(place, False, next_middle[0], both, [far_two, near_one, far_one])
    middle_two = products(place, True, next_middle[1], both, [middle_one])

    def late_sum(stack, steps):
        for step in steps:
            given = lax.ppermute(stack[1], "tensor", [(i, i ^ step) for i in range(4)])
            given, _ = after((given, middle_two))
            stack = (stack[0].astype(jnp.float32) + given.astype(jnp.float32)).astype(jnp.bfloat16)
        return stack

    near = jnp.concatenate([near_one, late_sum(near_two, (1, 2))], axis=1)
    far = jnp.concatenate([far_one, late_sum(far_two, (2, 1))], axis=1)
    middle_one = late_sum(middle_one, (2, 1))

    own, across, outside = [(p, p) for p in range(4)], [(1, 2), (2, 1)], [(1, 3), (2, 0)]
    parts = [
        [
            send_all(near, homeward(own, side)),
            send_all(far, homeward(outside, side)),
            send_all(middle_one, homeward(across, side)),
        ]
        for side in (0, 1)
    ]
    given = lax.ppermute(middle_two[1], "tensor", [(i, i ^ 1) for i in range(4)])
    given, parts = after((given, parts))
    last_sum = (middle_two[0].astype(jnp.float32) + given.astype(jnp.float32)).astype(jnp.bfloat16)
    for side in (0, 1):
        last = send_all(last_sum[0], homeward(across, side))
        last = last + send_all(last_sum[1], homeward(across, side, 1))
        near, far, first = parts[side]
        parts[side] = near + far + jnp.concatenate([first, last], axis=0)
    return (*prior, jnp.concatenate(parts, axis=1))


def solution(mesh):
    fits = mesh.shape["dp"] == 8 and mesh.shape["tensor"] == 4
    return jax.shard_map(
        body_planes if fits else body_general,
        mesh=mesh,
        in_specs=(
            P("dp", None),
            P("dp", "tensor"),
            P("dp"),
            P("dp", None),
            P("dp"),
            P("dp", "tensor"),
            P("dp", "tensor"),
            P("dp", "tensor"),
            P("dp", "tensor"),
        ),
        out_specs=(
            P("dp", "tensor"),
            P("dp", "tensor"),
            P("dp", "tensor"),
            P("dp", "tensor"),
            P("dp", "tensor"),
        ),
        check_vma=False,
    )
```

```python
import functools

import jax
import jax.numpy as jnp
from jax import lax
from jax.experimental import pallas as pl
from jax.experimental.pallas import tpu as pltpu
from jax.sharding import PartitionSpec as P

LEN = 32


beta_dpo = 0.1
beta_one = 0.9
beta_two = 0.999
bias_one = 1.0 - 0.9**10
bias_two = 1.0 - 0.999**10
adam_eps = 1e-08
rate_learn = 0.001

ROW_PARTS = ((0, 2), (2, 2), (4, 4))


def row_factors(ratios, pair_row, lengths):
    seq_count = ratios.shape[0]
    seq_slots = jnp.arange(seq_count, dtype=jnp.int32)
    chosen = pair_row[0::2]
    rejected = pair_row[1::2]
    pick_chosen = (chosen[:, None] == seq_slots[None, :]).astype(jnp.float32)
    pick_rejected = (rejected[:, None] == seq_slots[None, :]).astype(jnp.float32)
    margin = beta_dpo * (
        jnp.sum(pick_chosen * ratios[None, :], axis=1)
        - jnp.sum(pick_rejected * ratios[None, :], axis=1)
    )
    weight = beta_dpo * jax.nn.sigmoid(-margin)
    coefficient = jnp.sum(weight[:, None] * (pick_rejected - pick_chosen), axis=0)
    position = jnp.arange(LEN, dtype=jnp.int32)
    in_length = (position[None, :] < lengths[:, None]).astype(jnp.float32)
    return coefficient[:, None] * in_length


def scale_rows(out_grad, log_ratio, pair_order, seq_len):
    factors = row_factors(log_ratio, pair_order[0], seq_len)
    return (out_grad.astype(jnp.float32) * factors.reshape(-1)[:, None]).astype(jnp.bfloat16)


def adam(grad, master, moment, second):
    new_moment = beta_one * moment + (1.0 - beta_one) * grad
    new_second = beta_two * second + (1.0 - beta_two) * grad * grad
    update = (new_moment * (1.0 / bias_one)) / (
        jnp.sqrt(new_second * (1.0 / bias_two)) + adam_eps
    )
    new_master = master - rate_learn * update
    return new_master, new_moment, new_second, update


def body_general(
    out_grad, hidden_act, log_ratio, pair_order, seq_len, master, moment, second, next_act
):
    scaled = scale_rows(out_grad, log_ratio, pair_order, seq_len)
    mine = lax.all_to_all(scaled, "dp", split_axis=1, concat_axis=0, tiled=True)
    hidden = lax.all_gather(hidden_act, "dp", axis=0, tiled=True)
    grad = lax.dot_general(
        mine, hidden, (((0,), (0,)), ((), ())), preferred_element_type=jnp.float32
    )
    new_master, new_moment, new_second, update = adam(grad, master, moment, second)
    weights = lax.all_gather(new_master.astype(jnp.bfloat16), "dp", axis=0, tiled=True)
    partial_next = lax.dot_general(
        next_act, weights, (((1,), (1,)), ((), ())), preferred_element_type=jnp.float32
    )
    summed = lax.psum_scatter(
        partial_next.astype(jnp.bfloat16), "tensor", scatter_dimension=1, tiled=True
    )
    return (new_master, new_moment, new_second, update, summed)


def planes(pairs):
    return [(2 * a + core, 2 * b + core) for a, b in pairs for core in (0, 1)]


PAIR = planes([(0, 1), (1, 0), (2, 3), (3, 2)])
MIDDLE = planes([(1, 2), (2, 1)])
OUTWARD = planes([(1, 0), (2, 3)])
INWARD = planes([(0, 1), (3, 2)])


def homeward(pairs, core, flip=0):
    return [
        ((2 * a + core) * 4 + 2 * y + x, (2 * b + (y ^ flip)) * 4 + 2 * (a // 2) + x)
        for a, b in pairs
        for y in (0, 1)
        for x in (0, 1)
    ]


CORES = [(2 * z + core, 2 * z + 1 - core) for z in range(4) for core in (0, 1)]


def step_kernel(n_act, skip, *refs):
    scaled_ref, scaled_t = refs[0], refs[-1]
    acts = refs[1 : 1 + n_act]
    master_ref, moment_ref, second_ref = refs[1 + n_act : 4 + n_act]
    outs = refs[4 + n_act + skip : -1]
    tokens = acts[0].shape[0]

    @pl.when(pl.program_id(0) == 0)
    def _():
        scaled_t[...] = scaled_ref[...].T

    grad = None
    for i, act in enumerate(acts):
        term = jnp.dot(
            scaled_t[:, i * tokens : (i + 1) * tokens],
            act[...],
            preferred_element_type=jnp.float32,
        )
        grad = term if grad is None else grad + term
    new_master, new_moment, new_second, update = adam(
        grad, master_ref[...], moment_ref[...], second_ref[...]
    )
    outs[0][...] = new_master
    outs[1][...] = new_moment
    outs[2][...] = new_second
    outs[3][...] = update
    outs[4][...] = new_master.astype(jnp.bfloat16)


def step_rows(part, scaled_all, acts, master, moment, second, prior, behind):
    rows_all, cols = master.shape
    rows = rows_all // 8 * part[1]
    r = part[0] // part[1]
    tokens = acts[0].shape[0]
    tile = 768
    state = pl.BlockSpec((rows, tile), lambda t: (r, t))
    in_specs = (
        [pl.BlockSpec((scaled_all.shape[0], rows), lambda t: (0, r))]
        + [pl.BlockSpec((tokens, tile), lambda t: (0, t))] * len(acts)
        + [state] * 3
    )
    operands = [scaled_all, *acts, master, moment, second]
    aliases = {}
    if prior is not None:
        for i, array in enumerate(prior):
            aliases[len(operands)] = i
            operands.append(array)
            in_specs.append(pl.BlockSpec(memory_space=pl.ANY))
    for array in behind:
        operands.append(array)
        in_specs.append(pl.BlockSpec(memory_space=pl.ANY))
    full = jax.ShapeDtypeStruct((rows_all, cols), jnp.float32)
    outs = pl.pallas_call(
        functools.partial(step_kernel, len(acts), len(operands) - 4 - len(acts)),
        grid=(cols // tile,),
        in_specs=in_specs,
        out_specs=[state] * 4 + [pl.BlockSpec((rows, tile), lambda t: (0, t))],
        out_shape=[full] * 4 + [jax.ShapeDtypeStruct((rows, cols), jnp.bfloat16)],
        input_output_aliases=aliases,
        scratch_shapes=[pltpu.VMEM((rows, scaled_all.shape[0]), jnp.bfloat16)],
        compiler_params=pltpu.CompilerParams(vmem_limit_bytes=60 * 1024 * 1024),
        cost_estimate=SMALL,
        name="gradient_adam",
    )(*operands)
    return outs[:4], outs[4]


SMALL = pl.CostEstimate(flops=1000, bytes_accessed=1000, transcendentals=0)


def times(tokens, rows):
    return lax.dot_general(
        tokens, rows, (((1,), (1,)), ((), ())), preferred_element_type=jnp.float32
    ).astype(jnp.bfloat16)


def product_kernel(x_first, n_weights, tiles, place_ref, mine_ref, other_ref, *refs):
    weights = refs[:n_weights]
    out_ref, all_ref = refs[-2:]
    step = pl.program_id(0)

    @pl.when(step == 0)
    def _():
        first = 0
        for ref in weights:
            rows = ref.shape[0]
            all_ref[first : first + rows] = ref[...]
            first += rows

    def store(tokens_ref):
        out = times(tokens_ref[...], all_ref[...])
        give = place_ref[0]
        half = out.shape[1] // 2
        for at, block in ((give, out[:, :half]), (1 - give, out[:, half:])):
            if x_first:
                out_ref[at, 0] = block
            else:
                out_ref[0, at] = block

    pl.when(step < tiles)(functools.partial(store, mine_ref))
    pl.when(step >= tiles)(functools.partial(store, other_ref))


def products(place, x_first, tokens, weights, behind=()):
    count, cols = tokens[0].shape
    features = sum(block.shape[0] for block in weights) // 2
    tile = 256
    tiles = count // tile

    def out_map(t, place):
        y = jnp.where(t < tiles, place[1], 1 - place[1])
        return (0, y, t % tiles, 0) if x_first else (y, 0, t % tiles, 0)

    in_specs = [
        pl.BlockSpec((tile, cols), lambda t, place: (jnp.minimum(t, tiles - 1), 0)),
        pl.BlockSpec((tile, cols), lambda t, place: (jnp.maximum(t - tiles, 0), 0)),
    ]
    in_specs += [pl.BlockSpec(block.shape, lambda t, place: (0, 0)) for block in weights]
    in_specs += [pl.BlockSpec(memory_space=pl.ANY)] * len(behind)
    return pl.pallas_call(
        functools.partial(product_kernel, x_first, len(weights), tiles),
        grid_spec=pltpu.PrefetchScalarGridSpec(
            num_scalar_prefetch=1,
            grid=(2 * tiles,),
            in_specs=in_specs,
            out_specs=pl.BlockSpec(
                (2, 1, tile, features) if x_first else (1, 2, tile, features), out_map
            ),
            scratch_shapes=[pltpu.VMEM((2 * features, cols), jnp.bfloat16)],
        ),
        out_shape=jax.ShapeDtypeStruct((2, 2, count, features), jnp.bfloat16),
        compiler_params=pltpu.CompilerParams(vmem_limit_bytes=60 * 1024 * 1024),
        cost_estimate=SMALL,
        name="product",
    )(place, *tokens, *weights, *behind)


def add_step(stack, step):
    given = lax.ppermute(stack[1], "tensor", [(i, i ^ step) for i in range(4)])
    return (stack[0].astype(jnp.float32) + given.astype(jnp.float32)).astype(jnp.bfloat16)


def body_planes(
    out_grad, hidden_act, log_ratio, pair_order, seq_len, master, moment, second, next_act
):
    send = lambda array, pairs: lax.ppermute(array, "dp", pairs)
    after = lax.optimization_barrier
    send_all = lambda array, pairs: lax.ppermute(array, ("dp", "tensor"), pairs)
    k = lax.axis_index("dp")
    j = lax.axis_index("tensor")
    z, core = k // 2, k % 2
    inner = (z == 1) | (z == 2)
    tokens = hidden_act.shape[0]
    model = out_grad.shape[1]
    rows_all, cols = master.shape

    pair_act = send(hidden_act, PAIR)
    middle_act = send(hidden_act, MIDDLE)

    scaled = scale_rows(out_grad, log_ratio, pair_order, seq_len)
    share = tokens // 4
    width = model // 4
    part = lax.dynamic_slice_in_dim(scaled, j * share, share, 0)
    pieces = [lax.dynamic_slice_in_dim(part, (z ^ d) * width, width, 1) for d in range(4)]
    for d in (1, 2, 3):
        pieces[d] = send(pieces[d], planes([(p, p ^ d) for p in range(4)]))

    rows = next_act.shape[0] // 2
    next_parts = [next_act[:rows], next_act[rows:]]
    pair_act, middle_act, own_act, own_next, next_parts, pieces = after(
        (pair_act, middle_act, hidden_act, next_act, next_parts, pieces)
    )
    forward_act = send(pair_act, MIDDLE)
    far_one = send(middle_act, OUTWARD)
    inward, quarter = [], next_act.shape[0] // 4
    for i in range(4):
        part_next = own_next[i * quarter : (i + 1) * quarter]
        if inward:
            part_next, inward[-1] = after((part_next, inward[-1]))
        inward.append(send(part_next, INWARD))
    next_inward = jnp.concatenate(inward, axis=0)
    pieces = [
        pieces[0],
        pieces[1],
        jnp.where(inner, pieces[3], pieces[2]),
        jnp.where(inner, pieces[2], pieces[3]),
    ]
    pieces = jnp.stack(pieces)
    half = width // 2
    keep = lax.dynamic_slice_in_dim(pieces, core * half, half, 2)
    give = lax.dynamic_slice_in_dim(pieces, (1 - core) * half, half, 2)
    part = jnp.stack([keep, send(give, CORES)], axis=1).reshape(1, 8, share, half)
    x, y = j % 2, j // 2
    given = lax.ppermute(part, "tensor", [(i, i ^ 1) for i in range(4)])
    part = jnp.concatenate([jnp.where(x == 0, part, given), jnp.where(x == 0, given, part)], 0)
    given = lax.ppermute(part, "tensor", [(i, i ^ 2) for i in range(4)])
    own_swap = send(own_act, CORES)
    pair_act, own_swap = after((pair_act, own_swap))
    pair_swap = send(pair_act, CORES)

    forward_act, far_one, middle_act, own_next, next_parts, pair_swap, part = after(
        (forward_act, far_one, middle_act, own_next, next_parts, pair_swap, part)
    )
    far_two = send(forward_act, OUTWARD)
    next_middle = [send(array, MIDDLE) for array in next_parts]
    third = jnp.where(inner, middle_act, far_one)
    third, given = after((third, given))
    third_swap = send(third, CORES)
    whole = jnp.concatenate([jnp.where(y == 0, part, given), jnp.where(y == 0, given, part)], 0)
    scaled_all = whole.transpose(1, 0, 2, 3).reshape(8 * tokens, half)
    own_next, third_swap = after((own_next, third_swap))
    next_own = [next_act, send(own_next, CORES)]
    far_two, next_middle[0], scaled_all = after((far_two, next_middle[0], scaled_all))
    fourth = jnp.where(inner, forward_act, far_two)
    fourth_swap = send(fourth, CORES)
    acts = [hidden_act, own_swap, pair_act, pair_swap, third, third_swap, fourth, fourth_swap]

    next_far = send(next_inward, MIDDLE)

    place = jnp.stack([(z & 1) ^ x, core ^ y])
    prior, owns, pairs = None, [], []
    for part in ROW_PARTS:
        behind = pairs[:1] if len(owns) == 2 else [next_own[1], next_inward]
        prior, own = step_rows(part, scaled_all, acts, master, moment, second, prior, behind)
        owns.append(own)
        if len(owns) < 3:
            pairs.append(send(own, PAIR))
    last_rows = owns[2].shape[0] // 2
    pairs += [send(part, PAIR) for part in (owns[2][:last_rows], owns[2][last_rows:])]
    one, two = tuple(owns[:2] + pairs[:2]), (owns[2], *pairs[2:])
    both = tuple(owns + pairs)

    def swapped(array, behind):
        array, _ = after((array, behind))
        return [array, send(array, CORES)]

    def sum_behind(stack, steps, behinds):
        for step, behind in zip(steps, behinds):
            given = lax.ppermute(stack[1], "tensor", [(i, i ^ step) for i in range(4)])
            given, _ = after((given, behind))
            stack = (stack[0].astype(jnp.float32) + given.astype(jnp.float32)).astype(jnp.bfloat16)
        return stack

    near_one = products(place, True, next_own, one, owns[2:])
    next_far, pairs[2], _ = after((next_far, pairs[2], near_one))
    next_far = [next_far, send(next_far, CORES)]
    far_one = products(place, False, next_far, one, [near_one])
    near_two = products(place, True, next_own, two, [far_one])
    far_two = products(place, False, next_far, two, [near_two])
    near_one = sum_behind(near_one, (1, 2), (far_one, near_two))
    far_one = sum_behind(far_one, (2, 1), (near_two, far_two))
    next_middle[0] = swapped(next_middle[0], near_two)
    next_middle[1] = swapped(next_middle[1], far_two)
    middle_one = products(place, False, next_middle[0], both, [far_two])
    middle_two = products(place, True, next_middle[1], both, [middle_one, near_one, far_one])
    soon, late = (middle_one, middle_two), (middle_two, middle_two)
    near = jnp.concatenate([near_one, sum_behind(near_two, (1, 2), soon)], axis=1)
    far = jnp.concatenate([far_one, sum_behind(far_two, (2, 1), soon)], axis=1)
    middle_one = sum_behind(middle_one, (2, 1), late)

    own, across, outside = [(p, p) for p in range(4)], [(1, 2), (2, 1)], [(1, 3), (2, 0)]
    parts = [
        [
            send_all(near, homeward(own, side)),
            send_all(far, homeward(outside, side)),
            send_all(middle_one, homeward(across, side)),
        ]
        for side in (0, 1)
    ]
    given = lax.ppermute(middle_two[1], "tensor", [(i, i ^ 1) for i in range(4)])
    last_sum = (middle_two[0].astype(jnp.float32) + given.astype(jnp.float32)).astype(jnp.bfloat16)
    for side in (0, 1):
        last = send_all(last_sum[0], homeward(across, side))
        last = last + send_all(last_sum[1], homeward(across, side, 1))
        near, far, first = parts[side]
        parts[side] = near + far + jnp.concatenate([first, last], axis=0)
    return (*prior, jnp.concatenate(parts, axis=1))


def solution(mesh):
    fits = mesh.shape["dp"] == 8 and mesh.shape["tensor"] == 4
    return jax.shard_map(
        body_planes if fits else body_general,
        mesh=mesh,
        in_specs=(
            P("dp", None),
            P("dp", "tensor"),
            P("dp"),
            P("dp", None),
            P("dp"),
            P("dp", "tensor"),
            P("dp", "tensor"),
            P("dp", "tensor"),
            P("dp", "tensor"),
        ),
        out_specs=(
            P("dp", "tensor"),
            P("dp", "tensor"),
            P("dp", "tensor"),
            P("dp", "tensor"),
            P("dp", "tensor"),
        ),
        check_vma=False,
    )
```

```python
import functools

import jax
import jax.numpy as jnp
from jax import lax
from jax.experimental import pallas as pl
from jax.experimental.pallas import tpu as pltpu
from jax.sharding import PartitionSpec as P

LEN = 32


beta_dpo = 0.1
beta_one = 0.9
beta_two = 0.999
bias_one = 1.0 - 0.9**10
bias_two = 1.0 - 0.999**10
adam_eps = 1e-08
rate_learn = 0.001

ROW_PARTS = ((0, 2), (2, 2), (4, 4))


def row_factors(ratios, pair_row, lengths):
    seq_count = ratios.shape[0]
    seq_slots = jnp.arange(seq_count, dtype=jnp.int32)
    chosen = pair_row[0::2]
    rejected = pair_row[1::2]
    pick_chosen = (chosen[:, None] == seq_slots[None, :]).astype(jnp.float32)
    pick_rejected = (rejected[:, None] == seq_slots[None, :]).astype(jnp.float32)
    margin = beta_dpo * (
        jnp.sum(pick_chosen * ratios[None, :], axis=1)
        - jnp.sum(pick_rejected * ratios[None, :], axis=1)
    )
    weight = beta_dpo * jax.nn.sigmoid(-margin)
    coefficient = jnp.sum(weight[:, None] * (pick_rejected - pick_chosen), axis=0)
    position = jnp.arange(LEN, dtype=jnp.int32)
    in_length = (position[None, :] < lengths[:, None]).astype(jnp.float32)
    return coefficient[:, None] * in_length


def scale_rows(out_grad, log_ratio, pair_order, seq_len):
    factors = row_factors(log_ratio, pair_order[0], seq_len)
    return (out_grad.astype(jnp.float32) * factors.reshape(-1)[:, None]).astype(jnp.bfloat16)


def adam(grad, master, moment, second):
    new_moment = beta_one * moment + (1.0 - beta_one) * grad
    new_second = beta_two * second + (1.0 - beta_two) * grad * grad
    update = (new_moment * (1.0 / bias_one)) / (
        jnp.sqrt(new_second * (1.0 / bias_two)) + adam_eps
    )
    new_master = master - rate_learn * update
    return new_master, new_moment, new_second, update


def body_general(
    out_grad, hidden_act, log_ratio, pair_order, seq_len, master, moment, second, next_act
):
    scaled = scale_rows(out_grad, log_ratio, pair_order, seq_len)
    mine = lax.all_to_all(scaled, "dp", split_axis=1, concat_axis=0, tiled=True)
    hidden = lax.all_gather(hidden_act, "dp", axis=0, tiled=True)
    grad = lax.dot_general(
        mine, hidden, (((0,), (0,)), ((), ())), preferred_element_type=jnp.float32
    )
    new_master, new_moment, new_second, update = adam(grad, master, moment, second)
    weights = lax.all_gather(new_master.astype(jnp.bfloat16), "dp", axis=0, tiled=True)
    partial_next = lax.dot_general(
        next_act, weights, (((1,), (1,)), ((), ())), preferred_element_type=jnp.float32
    )
    summed = lax.psum_scatter(
        partial_next.astype(jnp.bfloat16), "tensor", scatter_dimension=1, tiled=True
    )
    return (new_master, new_moment, new_second, update, summed)


def planes(pairs):
    return [(2 * a + core, 2 * b + core) for a, b in pairs for core in (0, 1)]


PAIR = planes([(0, 1), (1, 0), (2, 3), (3, 2)])
MIDDLE = planes([(1, 2), (2, 1)])
OUTWARD = planes([(1, 0), (2, 3)])
INWARD = planes([(0, 1), (3, 2)])


def homeward(pairs, core, flip=0):
    return [
        ((2 * a + core) * 4 + 2 * y + x, (2 * b + (y ^ flip)) * 4 + 2 * (a // 2) + x)
        for a, b in pairs
        for y in (0, 1)
        for x in (0, 1)
    ]


CORES = [(2 * z + core, 2 * z + 1 - core) for z in range(4) for core in (0, 1)]


def step_kernel(n_act, skip, *refs):
    scaled_ref, scaled_t = refs[0], refs[-1]
    acts = refs[1 : 1 + n_act]
    master_ref, moment_ref, second_ref = refs[1 + n_act : 4 + n_act]
    outs = refs[4 + n_act + skip : -1]
    tokens = acts[0].shape[0]

    @pl.when(pl.program_id(0) == 0)
    def _():
        scaled_t[...] = scaled_ref[...].T

    grad = None
    for i, act in enumerate(acts):
        term = jnp.dot(
            scaled_t[:, i * tokens : (i + 1) * tokens],
            act[...],
            preferred_element_type=jnp.float32,
        )
        grad = term if grad is None else grad + term
    new_master, new_moment, new_second, update = adam(
        grad, master_ref[...], moment_ref[...], second_ref[...]
    )
    outs[0][...] = new_master
    outs[1][...] = new_moment
    outs[2][...] = new_second
    outs[3][...] = update
    outs[4][...] = new_master.astype(jnp.bfloat16)


def step_rows(part, scaled_all, acts, master, moment, second, prior, behind):
    rows_all, cols = master.shape
    rows = rows_all // 8 * part[1]
    r = part[0] // part[1]
    tokens = acts[0].shape[0]
    tile = 1280
    state = pl.BlockSpec((rows, tile), lambda t: (r, t))
    in_specs = (
        [pl.BlockSpec((scaled_all.shape[0], rows), lambda t: (0, r))]
        + [pl.BlockSpec((tokens, tile), lambda t: (0, t))] * len(acts)
        + [state] * 3
    )
    operands = [scaled_all, *acts, master, moment, second]
    aliases = {}
    if prior is not None:
        for i, array in enumerate(prior):
            aliases[len(operands)] = i
            operands.append(array)
            in_specs.append(pl.BlockSpec(memory_space=pl.ANY))
    for array in behind:
        operands.append(array)
        in_specs.append(pl.BlockSpec(memory_space=pl.ANY))
    full = jax.ShapeDtypeStruct((rows_all, cols), jnp.float32)
    outs = pl.pallas_call(
        functools.partial(step_kernel, len(acts), len(operands) - 4 - len(acts)),
        grid=(cols // tile,),
        in_specs=in_specs,
        out_specs=[state] * 4 + [pl.BlockSpec((rows, tile), lambda t: (0, t))],
        out_shape=[full] * 4 + [jax.ShapeDtypeStruct((rows, cols), jnp.bfloat16)],
        input_output_aliases=aliases,
        scratch_shapes=[pltpu.VMEM((rows, scaled_all.shape[0]), jnp.bfloat16)],
        compiler_params=pltpu.CompilerParams(vmem_limit_bytes=60 * 1024 * 1024),
        cost_estimate=SMALL,
        name="gradient_adam",
    )(*operands)
    return outs[:4], outs[4]


SMALL = pl.CostEstimate(flops=1000, bytes_accessed=1000, transcendentals=0)


def times(tokens, rows):
    return lax.dot_general(
        tokens, rows, (((1,), (1,)), ((), ())), preferred_element_type=jnp.float32
    ).astype(jnp.bfloat16)


def product_kernel(x_first, n_weights, tiles, place_ref, mine_ref, other_ref, *refs):
    weights = refs[:n_weights]
    out_ref, all_ref = refs[-2:]
    step = pl.program_id(0)

    @pl.when(step == 0)
    def _():
        first = 0
        for ref in weights:
            rows = ref.shape[0]
            all_ref[first : first + rows] = ref[...]
            first += rows

    def store(tokens_ref):
        out = times(tokens_ref[...], all_ref[...])
        give = place_ref[0]
        half = out.shape[1] // 2
        for at, block in ((give, out[:, :half]), (1 - give, out[:, half:])):
            if x_first:
                out_ref[at, 0] = block
            else:
                out_ref[0, at] = block

    pl.when(step < tiles)(functools.partial(store, mine_ref))
    pl.when(step >= tiles)(functools.partial(store, other_ref))


def products(place, x_first, tokens, weights, behind=()):
    count, cols = tokens[0].shape
    features = sum(block.shape[0] for block in weights) // 2
    tile = 256
    tiles = count // tile

    def out_map(t, place):
        y = jnp.where(t < tiles, place[1], 1 - place[1])
        return (0, y, t % tiles, 0) if x_first else (y, 0, t % tiles, 0)

    in_specs = [
        pl.BlockSpec((tile, cols), lambda t, place: (jnp.minimum(t, tiles - 1), 0)),
        pl.BlockSpec((tile, cols), lambda t, place: (jnp.maximum(t - tiles, 0), 0)),
    ]
    in_specs += [pl.BlockSpec(block.shape, lambda t, place: (0, 0)) for block in weights]
    in_specs += [pl.BlockSpec(memory_space=pl.ANY)] * len(behind)
    return pl.pallas_call(
        functools.partial(product_kernel, x_first, len(weights), tiles),
        grid_spec=pltpu.PrefetchScalarGridSpec(
            num_scalar_prefetch=1,
            grid=(2 * tiles,),
            in_specs=in_specs,
            out_specs=pl.BlockSpec(
                (2, 1, tile, features) if x_first else (1, 2, tile, features), out_map
            ),
            scratch_shapes=[pltpu.VMEM((2 * features, cols), jnp.bfloat16)],
        ),
        out_shape=jax.ShapeDtypeStruct((2, 2, count, features), jnp.bfloat16),
        compiler_params=pltpu.CompilerParams(vmem_limit_bytes=60 * 1024 * 1024),
        cost_estimate=SMALL,
        name="product",
    )(place, *tokens, *weights, *behind)


def add_step(stack, step):
    given = lax.ppermute(stack[1], "tensor", [(i, i ^ step) for i in range(4)])
    return (stack[0].astype(jnp.float32) + given.astype(jnp.float32)).astype(jnp.bfloat16)


def body_planes(
    out_grad, hidden_act, log_ratio, pair_order, seq_len, master, moment, second, next_act
):
    send = lambda array, pairs: lax.ppermute(array, "dp", pairs)
    after = lax.optimization_barrier
    send_all = lambda array, pairs: lax.ppermute(array, ("dp", "tensor"), pairs)
    k = lax.axis_index("dp")
    j = lax.axis_index("tensor")
    z, core = k // 2, k % 2
    inner = (z == 1) | (z == 2)
    tokens = hidden_act.shape[0]
    model = out_grad.shape[1]
    rows_all, cols = master.shape

    pair_act = send(hidden_act, PAIR)
    middle_act = send(hidden_act, MIDDLE)

    scaled = scale_rows(out_grad, log_ratio, pair_order, seq_len)
    share = tokens // 4
    width = model // 4
    part = lax.dynamic_slice_in_dim(scaled, j * share, share, 0)
    pieces = [lax.dynamic_slice_in_dim(part, (z ^ d) * width, width, 1) for d in range(4)]
    for d in (1, 2, 3):
        pieces[d] = send(pieces[d], planes([(p, p ^ d) for p in range(4)]))

    rows = next_act.shape[0] // 2
    next_parts = [next_act[:rows], next_act[rows:]]
    pair_act, middle_act, own_act, own_next, next_parts, pieces = after(
        (pair_act, middle_act, hidden_act, next_act, next_parts, pieces)
    )
    forward_act = send(pair_act, MIDDLE)
    far_one = send(middle_act, OUTWARD)
    inward, quarter = [], next_act.shape[0] // 4
    for i in range(4):
        part_next = own_next[i * quarter : (i + 1) * quarter]
        if inward:
            part_next, inward[-1] = after((part_next, inward[-1]))
        inward.append(send(part_next, INWARD))
    next_inward = jnp.concatenate(inward, axis=0)
    pieces = [
        pieces[0],
        pieces[1],
        jnp.where(inner, pieces[3], pieces[2]),
        jnp.where(inner, pieces[2], pieces[3]),
    ]
    pieces = jnp.stack(pieces)
    half = width // 2
    keep = lax.dynamic_slice_in_dim(pieces, core * half, half, 2)
    give = lax.dynamic_slice_in_dim(pieces, (1 - core) * half, half, 2)
    part = jnp.stack([keep, send(give, CORES)], axis=1).reshape(1, 8, share, half)
    x, y = j % 2, j // 2
    given = lax.ppermute(part, "tensor", [(i, i ^ 1) for i in range(4)])
    part = jnp.concatenate([jnp.where(x == 0, part, given), jnp.where(x == 0, given, part)], 0)
    given = lax.ppermute(part, "tensor", [(i, i ^ 2) for i in range(4)])
    own_swap = send(own_act, CORES)
    pair_act, own_swap = after((pair_act, own_swap))
    pair_swap = send(pair_act, CORES)

    forward_act, far_one, middle_act, own_next, next_parts, pair_swap, part = after(
        (forward_act, far_one, middle_act, own_next, next_parts, pair_swap, part)
    )
    far_two = send(forward_act, OUTWARD)
    next_middle = [send(array, MIDDLE) for array in next_parts]
    third = jnp.where(inner, middle_act, far_one)
    third, given = after((third, given))
    third_swap = send(third, CORES)
    whole = jnp.concatenate([jnp.where(y == 0, part, given), jnp.where(y == 0, given, part)], 0)
    scaled_all = whole.transpose(1, 0, 2, 3).reshape(8 * tokens, half)
    own_next, third_swap = after((own_next, third_swap))
    next_own = [next_act, send(own_next, CORES)]
    far_two, next_middle[0], scaled_all = after((far_two, next_middle[0], scaled_all))
    fourth = jnp.where(inner, forward_act, far_two)
    fourth_swap = send(fourth, CORES)
    acts = [hidden_act, own_swap, pair_act, pair_swap, third, third_swap, fourth, fourth_swap]

    next_far = send(next_inward, MIDDLE)

    place = jnp.stack([(z & 1) ^ x, core ^ y])
    prior, owns, pairs = None, [], []
    for part in ROW_PARTS:
        behind = pairs[:1] if len(owns) == 2 else [next_own[1], next_inward]
        prior, own = step_rows(part, scaled_all, acts, master, moment, second, prior, behind)
        owns.append(own)
        if len(owns) < 3:
            pairs.append(send(own, PAIR))
    last_rows = owns[2].shape[0] // 2
    pairs += [send(part, PAIR) for part in (owns[2][:last_rows], owns[2][last_rows:])]
    one, two = tuple(owns[:2] + pairs[:2]), (owns[2], *pairs[2:])
    both = tuple(owns + pairs)

    def swapped(array, behind):
        array, _ = after((array, behind))
        return [array, send(array, CORES)]

    def sum_behind(stack, steps, behinds):
        for step, behind in zip(steps, behinds):
            given = lax.ppermute(stack[1], "tensor", [(i, i ^ step) for i in range(4)])
            given, _ = after((given, behind))
            stack = (stack[0].astype(jnp.float32) + given.astype(jnp.float32)).astype(jnp.bfloat16)
        return stack

    near_one = products(place, True, next_own, one, owns[2:])
    next_far, pairs[2], _ = after((next_far, pairs[2], near_one))
    next_far = [next_far, send(next_far, CORES)]
    far_one = products(place, False, next_far, one, [near_one])
    near_two = products(place, True, next_own, two, [far_one])
    far_two = products(place, False, next_far, two, [near_two])
    near_one = sum_behind(near_one, (1, 2), (far_one, near_two))
    far_one = sum_behind(far_one, (2, 1), (near_two, far_two))
    next_middle[0] = swapped(next_middle[0], near_two)
    next_middle[1] = swapped(next_middle[1], far_two)
    middle_one = products(place, False, next_middle[0], both, [far_two])
    middle_two = products(place, True, next_middle[1], both, [middle_one, near_one, far_one])
    soon, late = (middle_one, middle_two), (middle_two, middle_two)
    near = jnp.concatenate([near_one, sum_behind(near_two, (1, 2), soon)], axis=1)
    far = jnp.concatenate([far_one, sum_behind(far_two, (2, 1), soon)], axis=1)
    middle_one = sum_behind(middle_one, (2, 1), late)

    own, across, outside = [(p, p) for p in range(4)], [(1, 2), (2, 1)], [(1, 3), (2, 0)]
    parts = [
        [
            send_all(near, homeward(own, side)),
            send_all(far, homeward(outside, side)),
            send_all(middle_one, homeward(across, side)),
        ]
        for side in (0, 1)
    ]
    given = lax.ppermute(middle_two[1], "tensor", [(i, i ^ 1) for i in range(4)])
    last_sum = (middle_two[0].astype(jnp.float32) + given.astype(jnp.float32)).astype(jnp.bfloat16)
    for side in (0, 1):
        last = send_all(last_sum[0], homeward(across, side))
        last = last + send_all(last_sum[1], homeward(across, side, 1))
        near, far, first = parts[side]
        parts[side] = near + far + jnp.concatenate([first, last], axis=0)
    return (*prior, jnp.concatenate(parts, axis=1))


def solution(mesh):
    fits = mesh.shape["dp"] == 8 and mesh.shape["tensor"] == 4
    return jax.shard_map(
        body_planes if fits else body_general,
        mesh=mesh,
        in_specs=(
            P("dp", None),
            P("dp", "tensor"),
            P("dp"),
            P("dp", None),
            P("dp"),
            P("dp", "tensor"),
            P("dp", "tensor"),
            P("dp", "tensor"),
            P("dp", "tensor"),
        ),
        out_specs=(
            P("dp", "tensor"),
            P("dp", "tensor"),
            P("dp", "tensor"),
            P("dp", "tensor"),
            P("dp", "tensor"),
        ),
        check_vma=False,
    )
```
